32 devices in a mesh: dp: 8 (over z, x), group: 4 (over y, core).
Axes of the slice: x: 2, y: 2, z: 4, core: 2. Of those that a mesh axis runs over, the one named last changes fastest.
Arguments:
- inputs: float32 [8, 1024, 768], P('dp', 'group'), may hold values from -4 to 4
- segments: int32 [8, 1024], P('dp', 'group'), may hold values from 0 to 3, never falling along the last dimension, each value on 1 to 512 neighbouring positions
- grad_output: float32 [8, 1024, 768], P('dp', 'group'), may hold values from -6 to 6
- attend_weight: float32 [768, 2304], P(('dp', 'group')), may hold values from -0.21875 to 0.21875
- merge_weight: float32 [768, 768], P(('dp', 'group')), may hold values from -1.75 to 1.75
- expand_weight: float32 [768, 3072], P(('dp', 'group')), may hold values from -0.21875 to 0.21875
- shrink_weight: float32 [3072, 768], P(('dp', 'group')), may hold values from -0.109375 to 0.109375
- norm_gains: float32 [768, 2], P(('dp', 'group')), may hold values from 0.1 to 1.9
- bias_table: float32 [768, 6], P(('dp', 'group')), may hold values from -3 to 3
- expand_bias: float32 [3072], P(('dp', 'group')), may hold values from -3 to 3
- attend_mean: float32 [768, 2304], P(('dp', 'group')), may hold values from -0.06 to 0.06
- merge_mean: float32 [768, 768], P(('dp', 'group')), may hold values from -0.09 to 0.09
- expand_mean: float32 [768, 3072], P(('dp', 'group')), may hold values from -0.24 to 0.24
- shrink_mean: float32 [3072, 768], P(('dp', 'group')), may hold values from -0.42 to 0.42
- gains_mean: float32 [768, 2], P(('dp', 'group')), may hold values from -1.2 to 1.2
- table_mean: float32 [768, 6], P(('dp', 'group')), may hold values from -1.2 to 1.2
- bias_mean: float32 [3072], P(('dp', 'group')), may hold values from -0.24 to 0.24
- attend_square: float32 [768, 2304], P(('dp', 'group')), may hold values from 1e-06 to 8e-06
- merge_square: float32 [768, 768], P(('dp', 'group')), may hold values from 2e-06 to 1.6e-05
- expand_square: float32 [768, 3072], P(('dp', 'group')), may hold values from 1.5e-05 to 0.00012
- shrink_square: float32 [3072, 768], P(('dp', 'group')), may hold values from 5e-05 to 0.0004
- gains_square: float32 [768, 2], P(('dp', 'group')), may hold values from 0.0002 to 0.0016
- table_square: float32 [768, 6], P(('dp', 'group')), may hold values from 0.0002 to 0.0016
- bias_square: float32 [3072], P(('dp', 'group')), may hold values from 1.5e-05 to 0.00012
Outputs:
- block_output: float32 [8, 1024, 768], P('dp', 'group')
- input_grad: float32 [8, 1024, 768], P('dp', 'group')
- attend_grad: float32 [768, 2304], P(('dp', 'group'))
- merge_grad: float32 [768, 768], P(('dp', 'group'))
- expand_grad: float32 [768, 3072], P(('dp', 'group'))
- shrink_grad: float32 [3072, 768], P(('dp', 'group'))
- gains_grad: float32 [768, 2], P(('dp', 'group'))
- table_grad: float32 [768, 6], P(('dp', 'group'))
- bias_grad: float32 [3072], P(('dp', 'group'))
- attend_update: float32 [768, 2304], P(('dp', 'group'))
- merge_update: float32 [768, 768], P(('dp', 'group'))
- expand_update: float32 [768, 3072], P(('dp', 'group'))
- shrink_update: float32 [3072, 768], P(('dp', 'group'))
- gains_update: float32 [768, 2], P(('dp', 'group'))
- table_update: float32 [768, 6], P(('dp', 'group'))
- bias_update: float32 [3072], P(('dp', 'group'))
- attend_average: float32 [768, 2304], P(('dp', 'group'))
- merge_average: float32 [768, 768], P(('dp', 'group'))
- expand_average: float32 [768, 3072], P(('dp', 'group'))
- shrink_average: float32 [3072, 768], P(('dp', 'group'))
- gains_average: float32 [768, 2], P(('dp', 'group'))
- table_average: float32 [768, 6], P(('dp', 'group'))
- bias_average: float32 [3072], P(('dp', 'group'))
- attend_variance: float32 [768, 2304], P(('dp', 'group'))
- merge_variance: float32 [768, 768], P(('dp', 'group'))
- expand_variance: float32 [768, 3072], P(('dp', 'group'))
- shrink_variance: float32 [3072, 768], P(('dp', 'group'))
- gains_variance: float32 [768, 2], P(('dp', 'group'))
- table_variance: float32 [768, 6], P(('dp', 'group'))
- bias_variance: float32 [3072], P(('dp', 'group'))
The draws below stay inside these ranges and needn't reach their ends.
All inputs are finite; a program needn't handle non-finite values.
Results may differ from the reference program's by a relative error of at most 0.014.
The reference program's roundings to bfloat16 on the way count: a program that leaves them out, or rounds other values in their place, can miss the bound.
Values may be sent and summed in bfloat16 or wider, within the bound.
A program may use at most 192 MiB of HBM per device.

```python
import math
import jax
import jax.numpy as jnp
import numpy as np
from jax import lax

D = 768
FF = 3072
HEADS = 12
HEAD_DIM = 64
DOCS = 4
SEQ_LEN = 1024
NSEQ = 8
TOKENS = 8192


def draw_inputs(key, part):
    return jnp.clip(jax.random.normal(jax.random.fold_in(key, 5), (NSEQ, SEQ_LEN, D), jnp.float32), -4.0, 4.0)


def level_of(stream_key, shape, shards, least, largest):
    def one(position, parts):
        steps = jax.random.uniform(jax.random.fold_in(jax.random.fold_in(stream_key, 6), position), (parts,), jnp.float32, least / len(shards), largest / len(shards))
        return jnp.repeat(jnp.exp(steps), shape[position] // parts).reshape((-1,) + (1,) * (len(shape) - position - 1))

    loudness = one(*shards[0])
    for cut in shards[1:]:
        loudness = loudness * one(*cut)
    return loudness


def profile(number_of, total, limit, skew):
    portions = [(1 << 20) // math.isqrt(standing ** skew) + 1 for standing in range(2, number_of + 1)]
    rest, given = total - limit - (number_of - 1), [1] * (number_of - 1)
    while rest > 0:
        movable = [i for i in range(number_of - 1) if given[i] < limit]
        whole, left = sum([portions[i] for i in movable]), rest
        for i in movable:
            addition = min(limit - given[i], max(1, left * portions[i] // whole), rest)
            given[i] = given[i] + addition
            rest = rest - addition
    return np.array([limit] + given)


def uneven(stream_key, count, total, most, slope):
    if count == 2:
        one = jax.random.randint(stream_key, (), max(1, total - most), min(most, total - 1) + 1)
        return jnp.stack([one, total - one])
    sizes = jnp.asarray(profile(count, total, most, slope), jnp.int32)
    pairs = (count - 1) // 2
    giver, taker = sizes[1:1 + 2 * pairs:2], sizes[2:2 + 2 * pairs:2]
    margin = jnp.minimum(giver - 1, most - taker)
    passed = jax.random.randint(jax.random.fold_in(stream_key, 1), (pairs,), 0, 1 << 20) % (margin + 1)
    sizes = sizes.at[1:1 + 2 * pairs:2].set(giver - passed).at[2:2 + 2 * pairs:2].set(taker + passed)
    return sizes[jax.random.permutation(jax.random.fold_in(stream_key, 2), count)]


def scatter_about(stream_key, extent, deviation, limit, cuts=(), dtype=jnp.bfloat16):
    values = jax.random.normal(stream_key, extent, jnp.float32) * deviation
    if len(cuts) > 0:
        values = level_of(stream_key, extent, cuts, -0.22, 0.18) * values
    return jnp.clip(values, min=-limit, max=limit).astype(dtype)


def setup_inputs(seed: int = 0) -> dict:
    splits = jax.random.split(jax.random.key(seed), 25)
    return {
        "inputs": draw_inputs(jax.random.fold_in(splits[24], 71), 0),
        "segments": jax.vmap(lambda own: jnp.searchsorted(jnp.cumsum(uneven(own, DOCS, SEQ_LEN, SEQ_LEN // 2, 1)), jnp.arange(SEQ_LEN), side="right"))(jax.random.split(splits[1], NSEQ)).reshape((NSEQ, SEQ_LEN)).astype(jnp.int32),
        "grad_output": scatter_about(splits[2], (NSEQ, SEQ_LEN, D), 1.0, 6.0, ((0, 8), (1, 4)), jnp.float32),
        "attend_weight": scatter_about(splits[3], (D, 3 * D), D ** -0.5, 0.21875, ((0, 32),), jnp.float32),
        "merge_weight": scatter_about(splits[4], (D, D), (D // 64) ** -0.5, 1.75, ((0, 32),), jnp.float32),
        "expand_weight": scatter_about(splits[5], (D, FF), D ** -0.5, 0.21875, ((0, 32),), jnp.float32),
        "shrink_weight": scatter_about(splits[6], (FF, D), FF ** -0.5, 0.109375, ((0, 32),), jnp.float32),
        "norm_gains": jnp.clip(1.0 + 0.18 * jax.random.normal(splits[7], (D, 2), jnp.float32), 0.1, 1.9),
        "bias_table": scatter_about(splits[8], (D, 6), 0.5, 3.0, ((0, 32),), jnp.float32),
        "expand_bias": scatter_about(splits[9], (FF,), 0.5, 3.0, ((0, 32),), jnp.float32),
        "attend_mean": scatter_about(splits[10], (D, 3 * D), 0.01, 0.06, ((0, 32),), jnp.float32),
        "merge_mean": scatter_about(splits[11], (D, D), 0.015, 0.09, ((0, 32),), jnp.float32),
        "expand_mean": scatter_about(splits[12], (D, FF), 0.04, 0.24, ((0, 32),), jnp.float32),
        "shrink_mean": scatter_about(splits[13], (FF, D), 0.07, 0.42, ((0, 32),), jnp.float32),
        "gains_mean": scatter_about(splits[14], (D, 2), 0.2, 1.2, ((0, 32),), jnp.float32),
        "table_mean": scatter_about(splits[15], (D, 6), 0.2, 1.2, ((0, 32),), jnp.float32),
        "bias_mean": scatter_about(splits[16], (FF,), 0.04, 0.24, ((0, 32),), jnp.float32),
        "attend_square": jnp.clip(jnp.exp(math.log(7.999999979801942e-06) - 2.0794415 * jax.random.uniform(splits[17], (D, 3 * D), jnp.float32) ** level_of(splits[17], (D, 3 * D), ((0, 32),), -0.2, 0.2)), 9.999999974752427e-07, 7.999999979801942e-06),
        "merge_square": jnp.clip(jnp.exp(math.log(1.5999999959603883e-05) - 2.0794415 * jax.random.uniform(splits[18], (D, D), jnp.float32) ** level_of(splits[18], (D, D), ((0, 32),), -0.2, 0.2)), 1.9999999949504854e-06, 1.5999999959603883e-05),
        "expand_square": jnp.clip(jnp.exp(math.log(0.00012) - 2.0794415 * jax.random.uniform(splits[19], (D, FF), jnp.float32) ** level_of(splits[19], (D, FF), ((0, 32),), -0.2, 0.2)), 1.4999999621068127e-05, 0.00012),
        "shrink_square": jnp.clip(jnp.exp(math.log(0.0004) - 2.0794415 * jax.random.uniform(splits[20], (FF, D), jnp.float32) ** level_of(splits[20], (FF, D), ((0, 32),), -0.2, 0.2)), 4.999999873689376e-05, 0.0004),
        "gains_square": jnp.clip(jnp.exp(math.log(0.0016) - 2.0794415 * jax.random.uniform(splits[21], (D, 2), jnp.float32) ** level_of(splits[21], (D, 2), ((0, 32),), -0.2, 0.2)), 0.0002, 0.0016),
        "table_square": jnp.clip(jnp.exp(math.log(0.0016) - 2.0794415 * jax.random.uniform(splits[22], (D, 6), jnp.float32) ** level_of(splits[22], (D, 6), ((0, 32),), -0.2, 0.2)), 0.0002, 0.0016),
        "bias_square": jnp.clip(jnp.exp(math.log(0.00012) - 2.0794415 * jax.random.uniform(splits[23], (FF,), jnp.float32) ** level_of(splits[23], (FF,), ((0, 32),), -0.2, 0.2)), 1.4999999621068127e-05, 0.00012),
    }


EPS_NORM = 1e-12
NEG_FILL = -1e+30
BETA_ONE = 0.9
BETA_TWO = 0.999
CORRECT_ONE = 1.0 - 0.9 ** 3
CORRECT_TWO = 1.0 - 0.999 ** 3
ADAM_EPS = 1e-08
MATRIX_RATE = 0.03
VECTOR_RATE = 0.2
MATRIX_DECAY = 0.01
SQRT_HALF = 0.7071067811865476
INV_ROOT_TAU = 0.3989422804014327

def contract(left, right, left_dim, right_dim):
    return lax.dot_general(left, right, (((left_dim,), (right_dim,)), ((), ())), preferred_element_type=jnp.float32)

def to_heads(matrix):
    return matrix.reshape(matrix.shape[0], HEADS, HEAD_DIM).transpose(1, 0, 2)

def from_heads(stacked):
    return stacked.transpose(1, 0, 2).reshape(stacked.shape[1], HEADS * HEAD_DIM)

def gelu_parts(values):
    normal_cdf = 0.5 * (1.0 + lax.erf(values * SQRT_HALF))
    density = jnp.exp(-0.5 * values * values) * INV_ROOT_TAU
    return (values * normal_cdf, normal_cdf + values * density)

def norm_forward(values, gain, shift):
    center = values - lax.optimization_barrier(jnp.mean(values, axis=-1, keepdims=True))
    inverse = lax.rsqrt(lax.optimization_barrier(jnp.mean(center * center, axis=-1, keepdims=True)) + EPS_NORM)
    normed = center * inverse
    return (normed * gain + shift, normed, inverse)

def norm_backward(cotangent, normed, inverse, gain):
    scaled = cotangent * gain
    return inverse * (scaled - lax.optimization_barrier(jnp.mean(scaled, axis=-1, keepdims=True)) - normed * lax.optimization_barrier(jnp.mean(scaled * normed, axis=-1, keepdims=True)))

def masked_scores(query_one, key_one, same):
    scores = contract(query_one, key_one, 1, 1)
    return jnp.where(same, scores, NEG_FILL)

def heads_forward(query_heads, key_heads, value_heads, same):

    def one_head(operands):
        query_one, key_one, value_one = operands
        scores = masked_scores(query_one, key_one, same)
        highest = lax.optimization_barrier(jnp.max(scores, axis=1, keepdims=True))
        lse_rows = highest + jnp.log(lax.optimization_barrier(jnp.sum(jnp.exp(scores - highest), axis=1, keepdims=True)))
        probs = jnp.exp(scores - lse_rows).astype(jnp.bfloat16)
        context = jnp.dot(probs, value_one, preferred_element_type=jnp.float32)
        return (context.astype(jnp.bfloat16), lse_rows)
    return lax.map(one_head, (query_heads, key_heads, value_heads))

def heads_backward(query_heads, key_heads, value_heads, same, lse_heads, context_heads, dcontext_heads):

    def one_head(operands):
        query_one, key_one, value_one, lse_rows, context_one, dcontext = operands
        probs = jnp.exp(masked_scores(query_one, key_one, same) - lse_rows)
        probs_low = probs.astype(jnp.bfloat16)
        delta_rows = lax.optimization_barrier(jnp.sum(dcontext.astype(jnp.float32) * context_one.astype(jnp.float32), axis=1, keepdims=True))
        grad_probs = contract(dcontext, value_one, 1, 1)
        grad_scores = (probs * (grad_probs - delta_rows)).astype(jnp.bfloat16)
        grad_query = jnp.dot(grad_scores, key_one, preferred_element_type=jnp.float32) * 0.125
        grad_key = contract(grad_scores, query_one, 0, 0)
        grad_value = contract(probs_low, dcontext, 0, 0)
        return (grad_query, grad_key, grad_value)
    return lax.map(one_head, (query_heads, key_heads, value_heads, lse_heads, context_heads, dcontext_heads))

def layer_pass(working, inputs, segment, cotangent):
    attend_low, merge_low, expand_low, shrink_low, gains_low, table_low, bias_low = working
    gains_wide = gains_low.astype(jnp.float32)
    table_wide = table_low.astype(jnp.float32)
    bias_wide = bias_low.astype(jnp.float32)
    width = inputs.shape[1]
    source = inputs.astype(jnp.bfloat16)
    packed = jnp.dot(source, attend_low, preferred_element_type=jnp.float32)
    query = ((packed[:, :width] + table_wide[:, 2]) * 0.125).astype(jnp.bfloat16)
    keys = packed[:, width:2 * width].astype(jnp.bfloat16)
    values = (packed[:, 2 * width:] + table_wide[:, 3]).astype(jnp.bfloat16)
    same = segment[:, None] == segment[None, :]
    query_heads = to_heads(query)
    key_heads = to_heads(keys)
    value_heads = to_heads(values)
    context_heads, lse_heads = heads_forward(query_heads, key_heads, value_heads, same)
    context = from_heads(context_heads)
    first_sum = inputs + jnp.dot(context, merge_low, preferred_element_type=jnp.float32) + table_wide[:, 4]
    hidden_in, normed_one, inverse_one = norm_forward(first_sum, gains_wide[:, 0], table_wide[:, 0])
    hidden_low = hidden_in.astype(jnp.bfloat16)
    pre_act = jnp.dot(hidden_low, expand_low, preferred_element_type=jnp.float32) + bias_wide
    act_value, act_slope = gelu_parts(pre_act)
    activated = act_value.astype(jnp.bfloat16)
    second_sum = hidden_in + jnp.dot(activated, shrink_low, preferred_element_type=jnp.float32) + table_wide[:, 5]
    output, normed_two, inverse_two = norm_forward(second_sum, gains_wide[:, 1], table_wide[:, 1])
    gain_two = lax.optimization_barrier(jnp.sum(cotangent * normed_two, axis=0))
    shift_two = lax.optimization_barrier(jnp.sum(cotangent, axis=0))
    grad_second = norm_backward(cotangent, normed_two, inverse_two, gains_wide[:, 1])
    shrink_part = grad_second.astype(jnp.bfloat16)
    shrink_term = contract(activated, shrink_part, 0, 0)
    shrink_bias = lax.optimization_barrier(jnp.sum(grad_second, axis=0))
    grad_pre = contract(shrink_part, shrink_low, 1, 1) * act_slope
    expand_part = grad_pre.astype(jnp.bfloat16)
    expand_term = contract(hidden_low, expand_part, 0, 0)
    expand_bias_term = lax.optimization_barrier(jnp.sum(grad_pre, axis=0))
    grad_hidden = grad_second + contract(expand_part, expand_low, 1, 1)
    gain_one = lax.optimization_barrier(jnp.sum(grad_hidden * normed_one, axis=0))
    shift_one = lax.optimization_barrier(jnp.sum(grad_hidden, axis=0))
    grad_first = norm_backward(grad_hidden, normed_one, inverse_one, gains_wide[:, 0])
    merge_part = grad_first.astype(jnp.bfloat16)
    merge_term = contract(context, merge_part, 0, 0)
    merge_bias = lax.optimization_barrier(jnp.sum(grad_first, axis=0))
    grad_context = contract(merge_part, merge_low, 1, 1).astype(jnp.bfloat16)
    grad_query_heads, grad_key_heads, grad_value_heads = heads_backward(query_heads, key_heads, value_heads, same, lse_heads, context_heads, to_heads(grad_context))
    grad_query = from_heads(grad_query_heads)
    grad_keys = from_heads(grad_key_heads)
    grad_values = from_heads(grad_value_heads)
    attend_part = jnp.concatenate([grad_query, grad_keys, grad_values], axis=1).astype(jnp.bfloat16)
    attend_term = contract(source, attend_part, 0, 0)
    input_grad = grad_first + contract(attend_part, attend_low, 1, 1)
    gains_term = jnp.stack([gain_one, gain_two], axis=1)
    table_term = jnp.stack([shift_one, shift_two, lax.optimization_barrier(jnp.sum(grad_query, axis=0)), lax.optimization_barrier(jnp.sum(grad_values, axis=0)), merge_bias, shrink_bias], axis=1)
    return (output, input_grad, (attend_term, merge_term, expand_term, shrink_term, gains_term, table_term, expand_bias_term))

def adamw(weight, grad, first, second, rate, decay):
    first_new = BETA_ONE * first + (1.0 - BETA_ONE) * grad
    second_new = BETA_TWO * second + (1.0 - BETA_TWO) * grad * grad
    step_dir = first_new / CORRECT_ONE / (jnp.sqrt(second_new / CORRECT_TWO) + ADAM_EPS)
    return (weight - rate * (step_dir + decay * weight), first_new, second_new)

def reference(inputs, segments, grad_output, attend_weight, merge_weight, expand_weight, shrink_weight, norm_gains, bias_table, expand_bias, attend_mean, merge_mean, expand_mean, shrink_mean, gains_mean, table_mean, bias_mean, attend_square, merge_square, expand_square, shrink_square, gains_square, table_square, bias_square):
    owned = (attend_weight, merge_weight, expand_weight, shrink_weight, norm_gains, bias_table, expand_bias)
    working = tuple((piece.astype(jnp.bfloat16) for piece in owned))

    def per_sequence(totals, operands):
        source_rows, segment_row, cotangent = operands
        output, input_part, terms = layer_pass(working, source_rows, segment_row, cotangent)
        return (tuple((left + right for left, right in zip(totals, terms))), (output, input_part))
    zeros = tuple((jnp.zeros(piece.shape, jnp.float32) for piece in owned))
    totals, (outputs, input_grads) = lax.scan(per_sequence, zeros, (inputs, segments, grad_output))
    scale = 1.0 / math.sqrt(TOKENS)
    grads = tuple((total * scale for total in totals))
    means = (attend_mean, merge_mean, expand_mean, shrink_mean, gains_mean, table_mean, bias_mean)
    squares = (attend_square, merge_square, expand_square, shrink_square, gains_square, table_square, bias_square)
    rates = (MATRIX_RATE, MATRIX_RATE, MATRIX_RATE, MATRIX_RATE, VECTOR_RATE, VECTOR_RATE, VECTOR_RATE)
    decays = (MATRIX_DECAY, MATRIX_DECAY, MATRIX_DECAY, MATRIX_DECAY, 0.0, 0.0, 0.0)
    results = [adamw(owned[index], grads[index], means[index], squares[index], rates[index], decays[index]) for index in range(7)]
    updates = [result[0] for result in results]
    averages = [result[1] for result in results]
    variances = [result[2] for result in results]
    return (outputs, input_grads, grads[0], grads[1], grads[2], grads[3], grads[4], grads[5], grads[6], updates[0], updates[1], updates[2], updates[3], updates[4], updates[5], updates[6], averages[0], averages[1], averages[2], averages[3], averages[4], averages[5], averages[6], variances[0], variances[1], variances[2], variances[3], variances[4], variances[5], variances[6])
```

```python
import math

import jax
import jax.numpy as jnp
from jax import lax
from jax.sharding import PartitionSpec as P

HEADS = 12
HEAD_DIM = 64


EPS_NORM = 1e-12
NEG_FILL = -1e30
BETA_ONE = 0.9
BETA_TWO = 0.999
CORRECT_ONE = 1.0 - 0.9**3
CORRECT_TWO = 1.0 - 0.999**3
ADAM_EPS = 1e-08
MATRIX_RATE = 0.03
VECTOR_RATE = 0.2
MATRIX_DECAY = 0.01
SQRT_HALF = 0.7071067811865476
INV_ROOT_TAU = 0.3989422804014327


def axis_bits(name):
    size = lax.axis_size(name)
    return [(name, mask) for mask in (1 << step for step in range(size.bit_length() - 1))]


def shard_bits():
    return axis_bits("dp")[::-1] + axis_bits("group")[::-1]


def swap(array, name, mask):
    size = lax.axis_size(name)
    return lax.ppermute(array, name, [(place, place ^ mask) for place in range(size)])


def doubled(array, bits, order):
    rows, columns = array.shape
    held = array.reshape((1,) * len(bits) + (rows, columns))
    for position in order:
        name, mask = bits[position]
        other = swap(held, name, mask)
        upper = (lax.axis_index(name) & mask) != 0
        held = jnp.concatenate(
            [jnp.where(upper, other, held), jnp.where(upper, held, other)], axis=position
        )
    return held.reshape(-1, columns)


def halved(array, bits, order, sent):
    rows, columns = array.shape
    held = array.reshape((2,) * len(bits) + (rows >> len(bits), columns))
    for position in order:
        name, mask = bits[position]
        upper = ((lax.axis_index(name) & mask) != 0).astype(jnp.int32)
        parting = lax.dynamic_slice_in_dim(held, 1 - upper, 1, position).astype(sent)
        staying = lax.dynamic_slice_in_dim(held, upper, 1, position)
        held = staying + swap(parting, name, mask).astype(jnp.float32)
    return held.reshape(-1, columns)


def contract(left, right, left_dim, right_dim):
    return lax.dot_general(
        left, right, (((left_dim,), (right_dim,)), ((), ())), preferred_element_type=jnp.float32
    )


def to_heads(matrix):
    return matrix.reshape(matrix.shape[0], HEADS, HEAD_DIM).transpose(1, 0, 2)


def from_heads(stacked):
    return stacked.transpose(1, 0, 2).reshape(stacked.shape[1], HEADS * HEAD_DIM)


def gelu_parts(values):
    normal_cdf = 0.5 * (1.0 + lax.erf(values * SQRT_HALF))
    density = jnp.exp(-0.5 * values * values) * INV_ROOT_TAU
    return (values * normal_cdf, normal_cdf + values * density)


def norm_forward(values, gain, shift):
    center = values - jnp.mean(values, axis=-1, keepdims=True)
    inverse = lax.rsqrt(jnp.mean(center * center, axis=-1, keepdims=True) + EPS_NORM)
    normed = center * inverse
    return (normed * gain + shift, normed, inverse)


def norm_backward(cotangent, normed, inverse, gain):
    scaled = cotangent * gain
    return inverse * (
        scaled
        - jnp.mean(scaled, axis=-1, keepdims=True)
        - normed * jnp.mean(scaled * normed, axis=-1, keepdims=True)
    )


def masked_scores(query_one, key_one, same):
    scores = contract(query_one, key_one, 1, 1)
    return jnp.where(same, scores, NEG_FILL)


def heads_forward(query_heads, key_heads, value_heads, same):

    def one_head(operands):
        query_one, key_one, value_one = operands
        scores = masked_scores(query_one, key_one, same)
        highest = jnp.max(scores, axis=1, keepdims=True)
        lse_rows = highest + jnp.log(jnp.sum(jnp.exp(scores - highest), axis=1, keepdims=True))
        probs = jnp.exp(scores - lse_rows).astype(jnp.bfloat16)
        context = jnp.dot(probs, value_one, preferred_element_type=jnp.float32)
        return (context.astype(jnp.bfloat16), lse_rows)

    return lax.map(one_head, (query_heads, key_heads, value_heads))


def heads_query_grad(
    query_heads, key_heads, value_heads, same, lse_heads, delta_heads, dcontext_heads
):

    def one_head(operands):
        query_one, key_one, value_one, lse_rows, delta_rows, dcontext = operands
        probs = jnp.exp(masked_scores(query_one, key_one, same) - lse_rows)
        grad_probs = contract(dcontext, value_one, 1, 1)
        grad_scores = (probs * (grad_probs - delta_rows)).astype(jnp.bfloat16)
        return jnp.dot(grad_scores, key_one, preferred_element_type=jnp.float32) * 0.125

    return lax.map(
        one_head, (query_heads, key_heads, value_heads, lse_heads, delta_heads, dcontext_heads)
    )


def heads_key_side(query_heads, key_heads, value_heads, same, lse_cols, delta_cols, dcontext_heads):

    def one_head(operands):
        query_one, key_one, value_one, lse_row, delta_row, dcontext = operands
        probs_turned = jnp.exp(masked_scores(key_one, query_one, same) - lse_row)
        grad_turned = contract(value_one, dcontext, 1, 1)
        scores_grad = (probs_turned * (grad_turned - delta_row)).astype(jnp.bfloat16)
        grad_key = jnp.dot(scores_grad, query_one, preferred_element_type=jnp.float32)
        grad_value = jnp.dot(
            probs_turned.astype(jnp.bfloat16), dcontext, preferred_element_type=jnp.float32
        )
        return (grad_key, grad_value)

    return lax.map(
        one_head, (query_heads, key_heads, value_heads, lse_cols, delta_cols, dcontext_heads)
    )


def adamw(weight, grad, first, second, rate, decay):
    first_new = BETA_ONE * first + (1.0 - BETA_ONE) * grad
    second_new = BETA_TWO * second + (1.0 - BETA_TWO) * grad * grad
    step_dir = first_new / CORRECT_ONE / (jnp.sqrt(second_new / CORRECT_TWO) + ADAM_EPS)
    return (weight - rate * (step_dir + decay * weight), first_new, second_new)


def local(
    inputs,
    segments,
    grad_output,
    attend_weight,
    merge_weight,
    expand_weight,
    shrink_weight,
    norm_gains,
    bias_table,
    expand_bias,
    attend_mean,
    merge_mean,
    expand_mean,
    shrink_mean,
    gains_mean,
    table_mean,
    bias_mean,
    attend_square,
    merge_square,
    expand_square,
    shrink_square,
    gains_square,
    table_square,
    bias_square,
):
    wide_count = lax.axis_size("dp")
    narrow_count = lax.axis_size("group")
    bits = shard_bits()
    group_bits = axis_bits("group")[::-1]
    wide_bits = len(bits) - len(group_bits)
    far_first = list(range(wide_bits))
    tail = list(range(wide_bits, len(bits)))
    early_tail = tail[:-1]
    last = tail[-1:]
    gather_one = far_first + early_tail + last
    gather_two = far_first[:-1] + early_tail + far_first[-1:] + last
    small_own = jnp.concatenate([norm_gains, bias_table, expand_bias.reshape(-1, 4)], axis=1)
    small_own = jnp.pad(small_own, ((0, 0), (0, 128 - small_own.shape[1]))).astype(jnp.bfloat16)
    attend_small = doubled(
        jnp.concatenate([attend_weight.astype(jnp.bfloat16), small_own], axis=1), bits, gather_one
    )
    attend_columns = attend_weight.shape[1]
    attend_low = attend_small[:, :attend_columns]
    small_low = attend_small[:, attend_columns : attend_columns + 12]
    gains_low = small_low[:, :2]
    table_low = small_low[:, 2:8]
    bias_low = small_low[:, 8:12].reshape(-1)
    merge_low = doubled(merge_weight.astype(jnp.bfloat16), bits, gather_two)
    expand_low = doubled(expand_weight.astype(jnp.bfloat16), bits, gather_two)
    shrink_low = lax.all_gather(
        shrink_weight.astype(jnp.bfloat16), ("dp", "group"), axis=0, tiled=True
    )
    gains_wide = gains_low.astype(jnp.float32)
    table_wide = table_low.astype(jnp.float32)
    bias_wide = bias_low.astype(jnp.float32)
    rows_in = inputs[0]
    segment_own = segments[0]
    cotangent = grad_output[0]
    rows = rows_in.shape[0]
    width = rows_in.shape[1]
    source = rows_in.astype(jnp.bfloat16)
    packed = jnp.dot(source, attend_low, preferred_element_type=jnp.float32)
    query = ((packed[:, :width] + table_wide[:, 2]) * 0.125).astype(jnp.bfloat16)
    keys_own = packed[:, width : 2 * width].astype(jnp.bfloat16)
    values_own = (packed[:, 2 * width :] + table_wide[:, 3]).astype(jnp.bfloat16)
    both_all = doubled(jnp.concatenate([keys_own, values_own], axis=1), group_bits, [0, 1])
    keys_all, values_all = both_all[:, :width], both_all[:, width:]
    segment_all = doubled(segment_own[:, None], group_bits, [0, 1])[:, 0]
    same = segment_own[:, None] == segment_all[None, :]
    query_heads = to_heads(query)
    key_heads = to_heads(keys_all)
    value_heads = to_heads(values_all)
    context_heads, lse_heads = heads_forward(query_heads, key_heads, value_heads, same)
    context = from_heads(context_heads)
    first_sum = (
        rows_in + jnp.dot(context, merge_low, preferred_element_type=jnp.float32) + table_wide[:, 4]
    )
    hidden_in, normed_one, inverse_one = norm_forward(first_sum, gains_wide[:, 0], table_wide[:, 0])
    hidden_low = hidden_in.astype(jnp.bfloat16)
    pre_act = jnp.dot(hidden_low, expand_low, preferred_element_type=jnp.float32) + bias_wide
    act_value, act_slope = gelu_parts(pre_act)
    activated = act_value.astype(jnp.bfloat16)
    second_sum = (
        hidden_in
        + jnp.dot(activated, shrink_low, preferred_element_type=jnp.float32)
        + table_wide[:, 5]
    )
    output, normed_two, inverse_two = norm_forward(second_sum, gains_wide[:, 1], table_wide[:, 1])
    gain_two = jnp.sum(cotangent * normed_two, axis=0)
    shift_two = jnp.sum(cotangent, axis=0)
    grad_second = norm_backward(cotangent, normed_two, inverse_two, gains_wide[:, 1])
    shrink_part = grad_second.astype(jnp.bfloat16)
    shrink_term = contract(activated, shrink_part, 0, 0)
    shrink_bias = jnp.sum(grad_second, axis=0)
    grad_pre = contract(shrink_part, shrink_low, 1, 1) * act_slope
    expand_part = grad_pre.astype(jnp.bfloat16)
    expand_term = contract(hidden_low, expand_part, 0, 0)
    expand_bias_term = jnp.sum(grad_pre, axis=0)
    grad_hidden = grad_second + contract(expand_part, expand_low, 1, 1)
    gain_one = jnp.sum(grad_hidden * normed_one, axis=0)
    shift_one = jnp.sum(grad_hidden, axis=0)
    grad_first = norm_backward(grad_hidden, normed_one, inverse_one, gains_wide[:, 0])
    merge_part = grad_first.astype(jnp.bfloat16)
    merge_term = contract(context, merge_part, 0, 0)
    merge_bias = jnp.sum(grad_first, axis=0)
    grad_context = contract(merge_part, merge_low, 1, 1).astype(jnp.bfloat16)
    dcontext_heads = to_heads(grad_context)
    delta_heads = jnp.sum(
        dcontext_heads.astype(jnp.float32) * context_heads.astype(jnp.float32),
        axis=2,
        keepdims=True,
    )
    grad_query_heads = heads_query_grad(
        query_heads, key_heads, value_heads, same, lse_heads, delta_heads, dcontext_heads
    )
    grad_query = from_heads(grad_query_heads)
    query_all = doubled(query, group_bits, [0, 1])
    dcontext_all = doubled(grad_context, group_bits, [0, 1])
    rows_all = doubled(
        jnp.concatenate([lse_heads[:, :, 0].T, delta_heads[:, :, 0].T], axis=1), group_bits, [0, 1]
    )
    lse_all, delta_all = rows_all[:, :HEADS], rows_all[:, HEADS:]
    grad_key_heads, grad_value_heads = heads_key_side(
        to_heads(query_all),
        to_heads(keys_own),
        to_heads(values_own),
        same,
        lse_all.T[:, None, :],
        delta_all.T[:, None, :],
        to_heads(dcontext_all),
    )
    grad_keys = from_heads(grad_key_heads)
    grad_values = from_heads(grad_value_heads)
    attend_part = jnp.concatenate([grad_query, grad_keys, grad_values], axis=1).astype(jnp.bfloat16)
    attend_term = contract(source, attend_part, 0, 0)
    input_part = grad_first + contract(attend_part, attend_low, 1, 1)
    gains_term = jnp.stack([gain_one, gain_two], axis=1)
    table_term = jnp.stack(
        [
            shift_one,
            shift_two,
            jnp.sum(grad_query, axis=0),
            jnp.sum(grad_values, axis=0),
            merge_bias,
            shrink_bias,
        ],
        axis=1,
    )
    scatter_one = gather_one[::-1]
    scatter_two = gather_two[::-1]
    small_term = jnp.concatenate([gains_term, table_term, expand_bias_term.reshape(-1, 4)], axis=1)
    small_sum = halved(small_term, bits, scatter_one, jnp.float32)
    summed = (
        halved(attend_term, bits, scatter_one, jnp.bfloat16),
        halved(merge_term, bits, scatter_two, jnp.bfloat16),
        halved(expand_term, bits, scatter_two, jnp.bfloat16),
        halved(shrink_term, bits, scatter_one, jnp.bfloat16),
        small_sum[:, :2],
        small_sum[:, 2:8],
        small_sum[:, 8:].reshape(-1),
    )
    scale = 1.0 / math.sqrt(wide_count * narrow_count * rows)
    grads = [piece * scale for piece in summed]
    owned = (
        attend_weight,
        merge_weight,
        expand_weight,
        shrink_weight,
        norm_gains,
        bias_table,
        expand_bias,
    )
    means = (attend_mean, merge_mean, expand_mean, shrink_mean, gains_mean, table_mean, bias_mean)
    squares = (
        attend_square,
        merge_square,
        expand_square,
        shrink_square,
        gains_square,
        table_square,
        bias_square,
    )
    rates = (
        MATRIX_RATE,
        MATRIX_RATE,
        MATRIX_RATE,
        MATRIX_RATE,
        VECTOR_RATE,
        VECTOR_RATE,
        VECTOR_RATE,
    )
    decays = (MATRIX_DECAY, MATRIX_DECAY, MATRIX_DECAY, MATRIX_DECAY, 0.0, 0.0, 0.0)
    results = [
        adamw(owned[index], grads[index], means[index], squares[index], rates[index], decays[index])
        for index in range(7)
    ]
    updates = [result[0] for result in results]
    averages = [result[1] for result in results]
    variances = [result[2] for result in results]
    return (
        output[None],
        input_part[None],
        grads[0],
        grads[1],
        grads[2],
        grads[3],
        grads[4],
        grads[5],
        grads[6],
        updates[0],
        updates[1],
        updates[2],
        updates[3],
        updates[4],
        updates[5],
        updates[6],
        averages[0],
        averages[1],
        averages[2],
        averages[3],
        averages[4],
        averages[5],
        averages[6],
        variances[0],
        variances[1],
        variances[2],
        variances[3],
        variances[4],
        variances[5],
        variances[6],
    )


def solution(mesh):
    return jax.shard_map(
        local,
        mesh=mesh,
        in_specs=(
            P("dp", "group", None),
            P("dp", "group"),
            P("dp", "group", None),
            P(("dp", "group"), None),
            P(("dp", "group"), None),
            P(("dp", "group"), None),
            P(("dp", "group"), None),
            P(("dp", "group"), None),
            P(("dp", "group"), None),
            P(("dp", "group")),
            P(("dp", "group"), None),
            P(("dp", "group"), None),
            P(("dp", "group"), None),
            P(("dp", "group"), None),
            P(("dp", "group"), None),
            P(("dp", "group"), None),
            P(("dp", "group")),
            P(("dp", "group"), None),
            P(("dp", "group"), None),
            P(("dp", "group"), None),
            P(("dp", "group"), None),
            P(("dp", "group"), None),
            P(("dp", "group"), None),
            P(("dp", "group")),
        ),
        out_specs=(
            P("dp", "group", None),
            P("dp", "group", None),
            P(("dp", "group"), None),
            P(("dp", "group"), None),
            P(("dp", "group"), None),
            P(("dp", "group"), None),
            P(("dp", "group"), None),
            P(("dp", "group"), None),
            P(("dp", "group")),
            P(("dp", "group"), None),
            P(("dp", "group"), None),
            P(("dp", "group"), None),
            P(("dp", "group"), None),
            P(("dp", "group"), None),
            P(("dp", "group"), None),
            P(("dp", "group")),
            P(("dp", "group"), None),
            P(("dp", "group"), None),
            P(("dp", "group"), None),
            P(("dp", "group"), None),
            P(("dp", "group"), None),
            P(("dp", "group"), None),
            P(("dp", "group")),
            P(("dp", "group"), None),
            P(("dp", "group"), None),
            P(("dp", "group"), None),
            P(("dp", "group"), None),
            P(("dp", "group"), None),
            P(("dp", "group"), None),
            P(("dp", "group")),
        ),
        check_vma=False,
    )
```

```python
import math

import jax
import jax.numpy as jnp
from jax import lax
from jax.sharding import PartitionSpec as P

HEADS = 12
HEAD_DIM = 64


EPS_NORM = 1e-12
NEG_FILL = -1e30
BETA_ONE = 0.9
BETA_TWO = 0.999
CORRECT_ONE = 1.0 - 0.9**3
CORRECT_TWO = 1.0 - 0.999**3
ADAM_EPS = 1e-08
MATRIX_RATE = 0.03
VECTOR_RATE = 0.2
MATRIX_DECAY = 0.01
SQRT_HALF = 0.7071067811865476
INV_ROOT_TAU = 0.3989422804014327


def axis_bits(name):
    size = lax.axis_size(name)
    return [(name, mask) for mask in (1 << step for step in range(size.bit_length() - 1))]


def shard_bits():
    return axis_bits("dp")[::-1] + axis_bits("group")[::-1]


def swap(array, name, mask):
    size = lax.axis_size(name)
    return lax.ppermute(array, name, [(place, place ^ mask) for place in range(size)])


def doubled(array, bits, order):
    rows, columns = array.shape
    held = array.reshape((1,) * len(bits) + (rows, columns))
    for position in order:
        name, mask = bits[position]
        other = swap(held, name, mask)
        upper = (lax.axis_index(name) & mask) != 0
        held = jnp.concatenate(
            [jnp.where(upper, other, held), jnp.where(upper, held, other)], axis=position
        )
    return held.reshape(-1, columns)


def halved(array, bits, order, sent):
    rows, columns = array.shape
    held = array.reshape((2,) * len(bits) + (rows >> len(bits), columns))
    for position in order:
        name, mask = bits[position]
        upper = ((lax.axis_index(name) & mask) != 0).astype(jnp.int32)
        parting = lax.dynamic_slice_in_dim(held, 1 - upper, 1, position).astype(sent)
        staying = lax.dynamic_slice_in_dim(held, upper, 1, position)
        held = staying + swap(parting, name, mask).astype(jnp.float32)
    return held.reshape(-1, columns)


def contract(left, right, left_dim, right_dim):
    return lax.dot_general(
        left, right, (((left_dim,), (right_dim,)), ((), ())), preferred_element_type=jnp.float32
    )


def to_heads(matrix):
    return matrix.reshape(matrix.shape[0], HEADS, HEAD_DIM).transpose(1, 0, 2)


def from_heads(stacked):
    return stacked.transpose(1, 0, 2).reshape(stacked.shape[1], HEADS * HEAD_DIM)


def gelu_parts(values):
    normal_cdf = 0.5 * (1.0 + lax.erf(values * SQRT_HALF))
    density = jnp.exp(-0.5 * values * values) * INV_ROOT_TAU
    return (values * normal_cdf, normal_cdf + values * density)


def norm_forward(values, gain, shift):
    center = values - jnp.mean(values, axis=-1, keepdims=True)
    inverse = lax.rsqrt(jnp.mean(center * center, axis=-1, keepdims=True) + EPS_NORM)
    normed = center * inverse
    return (normed * gain + shift, normed, inverse)


def norm_backward(cotangent, normed, inverse, gain):
    scaled = cotangent * gain
    return inverse * (
        scaled
        - jnp.mean(scaled, axis=-1, keepdims=True)
        - normed * jnp.mean(scaled * normed, axis=-1, keepdims=True)
    )


def masked_scores(query_one, key_one, same):
    scores = contract(query_one, key_one, 1, 1)
    return jnp.where(same, scores, NEG_FILL)


def heads_forward(query_heads, key_heads, value_heads, same):

    def one_head(operands):
        query_one, key_one, value_one = operands
        scores = masked_scores(query_one, key_one, same)
        highest = jnp.max(scores, axis=1, keepdims=True)
        lse_rows = highest + jnp.log(jnp.sum(jnp.exp(scores - highest), axis=1, keepdims=True))
        probs = jnp.exp(scores - lse_rows).astype(jnp.bfloat16)
        context = jnp.dot(probs, value_one, preferred_element_type=jnp.float32)
        return (context.astype(jnp.bfloat16), lse_rows)

    return jax.vmap(one_head)((query_heads, key_heads, value_heads))


def heads_query_grad(
    query_heads, key_heads, value_heads, same, lse_heads, delta_heads, dcontext_heads
):

    def one_head(operands):
        query_one, key_one, value_one, lse_rows, delta_rows, dcontext = operands
        probs = jnp.exp(masked_scores(query_one, key_one, same) - lse_rows)
        grad_probs = contract(dcontext, value_one, 1, 1)
        grad_scores = (probs * (grad_probs - delta_rows)).astype(jnp.bfloat16)
        return jnp.dot(grad_scores, key_one, preferred_element_type=jnp.float32) * 0.125

    return jax.vmap(one_head)((query_heads, key_heads, value_heads, lse_heads, delta_heads, dcontext_heads))


def heads_key_side(query_heads, key_heads, value_heads, same, lse_cols, delta_cols, dcontext_heads):

    def one_head(operands):
        query_one, key_one, value_one, lse_row, delta_row, dcontext = operands
        probs_turned = jnp.exp(masked_scores(key_one, query_one, same) - lse_row)
        grad_turned = contract(value_one, dcontext, 1, 1)
        scores_grad = (probs_turned * (grad_turned - delta_row)).astype(jnp.bfloat16)
        grad_key = jnp.dot(scores_grad, query_one, preferred_element_type=jnp.float32)
        grad_value = jnp.dot(
            probs_turned.astype(jnp.bfloat16), dcontext, preferred_element_type=jnp.float32
        )
        return (grad_key, grad_value)

    return jax.vmap(one_head)((query_heads, key_heads, value_heads, lse_cols, delta_cols, dcontext_heads))


def adamw(weight, grad, first, second, rate, decay):
    first_new = BETA_ONE * first + (1.0 - BETA_ONE) * grad
    second_new = BETA_TWO * second + (1.0 - BETA_TWO) * grad * grad
    step_dir = first_new / CORRECT_ONE / (jnp.sqrt(second_new / CORRECT_TWO) + ADAM_EPS)
    return (weight - rate * (step_dir + decay * weight), first_new, second_new)


def local(
    inputs,
    segments,
    grad_output,
    attend_weight,
    merge_weight,
    expand_weight,
    shrink_weight,
    norm_gains,
    bias_table,
    expand_bias,
    attend_mean,
    merge_mean,
    expand_mean,
    shrink_mean,
    gains_mean,
    table_mean,
    bias_mean,
    attend_square,
    merge_square,
    expand_square,
    shrink_square,
    gains_square,
    table_square,
    bias_square,
):
    wide_count = lax.axis_size("dp")
    narrow_count = lax.axis_size("group")
    bits = shard_bits()
    group_bits = axis_bits("group")[::-1]
    wide_bits = len(bits) - len(group_bits)
    far_first = list(range(wide_bits))
    tail = list(range(wide_bits, len(bits)))
    early_tail = tail[:-1]
    last = tail[-1:]
    gather_one = far_first + early_tail + last
    gather_two = far_first[:-1] + early_tail + far_first[-1:] + last
    small_own = jnp.concatenate([norm_gains, bias_table, expand_bias.reshape(-1, 4)], axis=1)
    small_own = jnp.pad(small_own, ((0, 0), (0, 128 - small_own.shape[1]))).astype(jnp.bfloat16)
    attend_small = doubled(
        jnp.concatenate([attend_weight.astype(jnp.bfloat16), small_own], axis=1), bits, gather_one
    )
    attend_columns = attend_weight.shape[1]
    attend_low = attend_small[:, :attend_columns]
    small_low = attend_small[:, attend_columns : attend_columns + 12]
    gains_low = small_low[:, :2]
    table_low = small_low[:, 2:8]
    bias_low = small_low[:, 8:12].reshape(-1)
    merge_low = doubled(merge_weight.astype(jnp.bfloat16), bits, gather_two)
    expand_low = doubled(expand_weight.astype(jnp.bfloat16), bits, gather_two)
    shrink_low = lax.all_gather(
        shrink_weight.astype(jnp.bfloat16), ("dp", "group"), axis=0, tiled=True
    )
    gains_wide = gains_low.astype(jnp.float32)
    table_wide = table_low.astype(jnp.float32)
    bias_wide = bias_low.astype(jnp.float32)
    rows_in = inputs[0]
    segment_own = segments[0]
    cotangent = grad_output[0]
    rows = rows_in.shape[0]
    width = rows_in.shape[1]
    source = rows_in.astype(jnp.bfloat16)
    packed = jnp.dot(source, attend_low, preferred_element_type=jnp.float32)
    query = ((packed[:, :width] + table_wide[:, 2]) * 0.125).astype(jnp.bfloat16)
    keys_own = packed[:, width : 2 * width].astype(jnp.bfloat16)
    values_own = (packed[:, 2 * width :] + table_wide[:, 3]).astype(jnp.bfloat16)
    both_all = doubled(jnp.concatenate([keys_own, values_own], axis=1), group_bits, [0, 1])
    keys_all, values_all = both_all[:, :width], both_all[:, width:]
    segment_all = doubled(segment_own[:, None], group_bits, [0, 1])[:, 0]
    same = segment_own[:, None] == segment_all[None, :]
    query_heads = to_heads(query)
    key_heads = to_heads(keys_all)
    value_heads = to_heads(values_all)
    context_heads, lse_heads = heads_forward(query_heads, key_heads, value_heads, same)
    context = from_heads(context_heads)
    first_sum = (
        rows_in + jnp.dot(context, merge_low, preferred_element_type=jnp.float32) + table_wide[:, 4]
    )
    hidden_in, normed_one, inverse_one = norm_forward(first_sum, gains_wide[:, 0], table_wide[:, 0])
    hidden_low = hidden_in.astype(jnp.bfloat16)
    pre_act = jnp.dot(hidden_low, expand_low, preferred_element_type=jnp.float32) + bias_wide
    act_value, act_slope = gelu_parts(pre_act)
    activated = act_value.astype(jnp.bfloat16)
    second_sum = (
        hidden_in
        + jnp.dot(activated, shrink_low, preferred_element_type=jnp.float32)
        + table_wide[:, 5]
    )
    output, normed_two, inverse_two = norm_forward(second_sum, gains_wide[:, 1], table_wide[:, 1])
    gain_two = jnp.sum(cotangent * normed_two, axis=0)
    shift_two = jnp.sum(cotangent, axis=0)
    grad_second = norm_backward(cotangent, normed_two, inverse_two, gains_wide[:, 1])
    shrink_part = grad_second.astype(jnp.bfloat16)
    shrink_term = contract(activated, shrink_part, 0, 0)
    shrink_bias = jnp.sum(grad_second, axis=0)
    grad_pre = contract(shrink_part, shrink_low, 1, 1) * act_slope
    expand_part = grad_pre.astype(jnp.bfloat16)
    expand_term = contract(hidden_low, expand_part, 0, 0)
    expand_bias_term = jnp.sum(grad_pre, axis=0)
    grad_hidden = grad_second + contract(expand_part, expand_low, 1, 1)
    gain_one = jnp.sum(grad_hidden * normed_one, axis=0)
    shift_one = jnp.sum(grad_hidden, axis=0)
    grad_first = norm_backward(grad_hidden, normed_one, inverse_one, gains_wide[:, 0])
    merge_part = grad_first.astype(jnp.bfloat16)
    merge_term = contract(context, merge_part, 0, 0)
    merge_bias = jnp.sum(grad_first, axis=0)
    grad_context = contract(merge_part, merge_low, 1, 1).astype(jnp.bfloat16)
    dcontext_heads = to_heads(grad_context)
    delta_heads = jnp.sum(
        dcontext_heads.astype(jnp.float32) * context_heads.astype(jnp.float32),
        axis=2,
        keepdims=True,
    )
    grad_query_heads = heads_query_grad(
        query_heads, key_heads, value_heads, same, lse_heads, delta_heads, dcontext_heads
    )
    grad_query = from_heads(grad_query_heads)
    query_all = doubled(query, group_bits, [0, 1])
    dcontext_all = doubled(grad_context, group_bits, [0, 1])
    rows_all = doubled(
        jnp.concatenate([lse_heads[:, :, 0].T, delta_heads[:, :, 0].T], axis=1), group_bits, [0, 1]
    )
    lse_all, delta_all = rows_all[:, :HEADS], rows_all[:, HEADS:]
    grad_key_heads, grad_value_heads = heads_key_side(
        to_heads(query_all),
        to_heads(keys_own),
        to_heads(values_own),
        same,
        lse_all.T[:, None, :],
        delta_all.T[:, None, :],
        to_heads(dcontext_all),
    )
    grad_keys = from_heads(grad_key_heads)
    grad_values = from_heads(grad_value_heads)
    attend_part = jnp.concatenate([grad_query, grad_keys, grad_values], axis=1).astype(jnp.bfloat16)
    attend_term = contract(source, attend_part, 0, 0)
    input_part = grad_first + contract(attend_part, attend_low, 1, 1)
    gains_term = jnp.stack([gain_one, gain_two], axis=1)
    table_term = jnp.stack(
        [
            shift_one,
            shift_two,
            jnp.sum(grad_query, axis=0),
            jnp.sum(grad_values, axis=0),
            merge_bias,
            shrink_bias,
        ],
        axis=1,
    )
    scatter_one = gather_one[::-1]
    scatter_two = gather_two[::-1]
    small_term = jnp.concatenate([gains_term, table_term, expand_bias_term.reshape(-1, 4)], axis=1)
    small_sum = halved(small_term, bits, scatter_one, jnp.float32)
    summed = (
        halved(attend_term, bits, scatter_one, jnp.bfloat16),
        halved(merge_term, bits, scatter_two, jnp.bfloat16),
        halved(expand_term, bits, scatter_two, jnp.bfloat16),
        halved(shrink_term, bits, scatter_one, jnp.bfloat16),
        small_sum[:, :2],
        small_sum[:, 2:8],
        small_sum[:, 8:].reshape(-1),
    )
    scale = 1.0 / math.sqrt(wide_count * narrow_count * rows)
    grads = [piece * scale for piece in summed]
    owned = (
        attend_weight,
        merge_weight,
        expand_weight,
        shrink_weight,
        norm_gains,
        bias_table,
        expand_bias,
    )
    means = (attend_mean, merge_mean, expand_mean, shrink_mean, gains_mean, table_mean, bias_mean)
    squares = (
        attend_square,
        merge_square,
        expand_square,
        shrink_square,
        gains_square,
        table_square,
        bias_square,
    )
    rates = (
        MATRIX_RATE,
        MATRIX_RATE,
        MATRIX_RATE,
        MATRIX_RATE,
        VECTOR_RATE,
        VECTOR_RATE,
        VECTOR_RATE,
    )
    decays = (MATRIX_DECAY, MATRIX_DECAY, MATRIX_DECAY, MATRIX_DECAY, 0.0, 0.0, 0.0)
    results = [
        adamw(owned[index], grads[index], means[index], squares[index], rates[index], decays[index])
        for index in range(7)
    ]
    updates = [result[0] for result in results]
    averages = [result[1] for result in results]
    variances = [result[2] for result in results]
    return (
        output[None],
        input_part[None],
        grads[0],
        grads[1],
        grads[2],
        grads[3],
        grads[4],
        grads[5],
        grads[6],
        updates[0],
        updates[1],
        updates[2],
        updates[3],
        updates[4],
        updates[5],
        updates[6],
        averages[0],
        averages[1],
        averages[2],
        averages[3],
        averages[4],
        averages[5],
        averages[6],
        variances[0],
        variances[1],
        variances[2],
        variances[3],
        variances[4],
        variances[5],
        variances[6],
    )


def solution(mesh):
    return jax.shard_map(
        local,
        mesh=mesh,
        in_specs=(
            P("dp", "group", None),
            P("dp", "group"),
            P("dp", "group", None),
            P(("dp", "group"), None),
            P(("dp", "group"), None),
            P(("dp", "group"), None),
            P(("dp", "group"), None),
            P(("dp", "group"), None),
            P(("dp", "group"), None),
            P(("dp", "group")),
            P(("dp", "group"), None),
            P(("dp", "group"), None),
            P(("dp", "group"), None),
            P(("dp", "group"), None),
            P(("dp", "group"), None),
            P(("dp", "group"), None),
            P(("dp", "group")),
            P(("dp", "group"), None),
            P(("dp", "group"), None),
            P(("dp", "group"), None),
            P(("dp", "group"), None),
            P(("dp", "group"), None),
            P(("dp", "group"), None),
            P(("dp", "group")),
        ),
        out_specs=(
            P("dp", "group", None),
            P("dp", "group", None),
            P(("dp", "group"), None),
            P(("dp", "group"), None),
            P(("dp", "group"), None),
            P(("dp", "group"), None),
            P(("dp", "group"), None),
            P(("dp", "group"), None),
            P(("dp", "group")),
            P(("dp", "group"), None),
            P(("dp", "group"), None),
            P(("dp", "group"), None),
            P(("dp", "group"), None),
            P(("dp", "group"), None),
            P(("dp", "group"), None),
            P(("dp", "group")),
            P(("dp", "group"), None),
            P(("dp", "group"), None),
            P(("dp", "group"), None),
            P(("dp", "group"), None),
            P(("dp", "group"), None),
            P(("dp", "group"), None),
            P(("dp", "group")),
            P(("dp", "group"), None),
            P(("dp", "group"), None),
            P(("dp", "group"), None),
            P(("dp", "group"), None),
            P(("dp", "group"), None),
            P(("dp", "group"), None),
            P(("dp", "group")),
        ),
        check_vma=False,
    )
```
